256 devices in a mesh: cfg: 2 (over core), pipe: 16 (over y, x), sp: 8 (over z).
Axes of the slice: x: 4, y: 4, z: 8, core: 2. Of those that a mesh axis runs over, the one named last changes fastest.
Arguments:
- activations: bfloat16 [16, 2, 512, 3072], P('pipe', 'cfg', 'sp'), may hold values from -6 to 6
- w_qkv: bfloat16 [16, 3072, 3, 2048], P('pipe', None, None, ('cfg', 'sp')), may hold values from -0.109375 to 0.109375
- w_out: bfloat16 [16, 2048, 3072], P('pipe', ('cfg', 'sp')), may hold values from -0.125 to 0.125
- stash: bfloat16 [16, 2, 2, 4096, 2048], P('pipe', None, None, None, ('cfg', 'sp')), may hold values from -6 to 6
- qk_gain: float32 [16, 2, 128], P('pipe'), may hold values from 1.5 to 2.5
- modulation: bfloat16 [16, 30, 3, 3072], P('pipe'), may hold values from -4 to 4
- patch_slot: int32 [16], P('pipe'), may hold values from 0 to 7
- timestep: int32 [16], P('pipe'), may hold values from 0 to 29
Outputs:
- handed: bfloat16 [16, 2, 512, 3072], P('pipe', 'cfg', 'sp')
The draws below stay inside these ranges and needn't reach their ends.
All inputs are finite; a program needn't handle non-finite values.
Results may differ from the reference program's by a relative error of at most 0.017.
Values may be sent and summed in bfloat16 or wider, within the bound.
No kernel may reach another device: no remote copies, remote signals or barrier semaphores. Data moves between devices by JAX's collectives and lax.ppermute only.
A program may use at most 128 MiB of HBM per device.

```python
import math
import jax
import jax.numpy as jnp
from jax import lax

D = 3072
HEADS = 16
HD = 128
STASH = 4096
STEPS = 30
PATCH = 512
PIPE = 16
N_CFG = 2
N_SP = 8


def touch_ends(values, own_key, smallest, largest):
    spot = [jax.random.randint(jax.random.fold_in(own_key, axis), (), 0, length) for axis, length in enumerate(values.shape)]
    widest = values.shape.index(max(values.shape))
    next_to = spot[:widest] + [(spot[widest] + 1) % values.shape[widest]] + spot[widest + 1:]
    return values.at[tuple(spot)].set(smallest).at[tuple(next_to)].set(largest)


def level_of(stream_key, shape, cuts, least, high):
    factor_of = 1.0
    for position, shards_of in cuts:
        heights = jax.random.uniform(jax.random.fold_in(jax.random.fold_in(stream_key, 6), position), (shards_of,), jnp.float32, least / len(cuts), high / len(cuts))
        factor_of = factor_of * jnp.repeat(jnp.exp(heights), shape[position] // shards_of).reshape((-1,) + (1,) * (len(shape) - 1 - position))
    return factor_of


def centred(stream_key, extent, scale, limit, pieces=(), kind=jnp.bfloat16):
    values = scale * jax.random.normal(stream_key, extent, jnp.float32)
    if pieces:
        values = values * level_of(stream_key, extent, pieces, -0.22, 0.18)
    return jnp.clip(values, -limit, limit).astype(kind)


def setup_inputs(seed: int = 0) -> dict:
    splits = jax.random.split(jax.random.key(seed), 9)
    activations = centred(splits[0], (PIPE, 2, PATCH, D), 1.0, 6.0, ((0, 16), (1, 2), (2, 8)))
    w_qkv = centred(splits[1], (PIPE, D, 3, HEADS * HD), D ** -0.5, 0.109375, ((0, 16), (3, 16)))
    w_out = centred(splits[2], (PIPE, HEADS * HD, D), (HEADS * HD) ** -0.5, 0.125, ((0, 16), (1, 16)))
    stash = centred(splits[3], (PIPE, 2, 2, STASH, HEADS * HD), 1.0, 6.0, ((0, 16), (4, 16)))
    qk_gain = jnp.clip(jnp.exp(math.log(2.5) - 0.51082562 * jax.random.uniform(splits[4], (PIPE, 2, HD), jnp.float32) ** level_of(splits[4], (PIPE, 2, HD), ((0, 16),), -0.2, 0.2)), 1.5, 2.5)
    modulation = centred(splits[5], (PIPE, STEPS, 3, D), 1.0, 4.0, ((0, 16),))
    patch_slot = touch_ends(jax.random.randint(splits[6], (PIPE,), 0, STASH // PATCH), jax.random.fold_in(splits[6], 1), 0, (STASH // PATCH) - 1).astype(jnp.int32)
    timestep = touch_ends(jax.random.randint(splits[7], (PIPE,), 0, STEPS), jax.random.fold_in(splits[7], 1), 0, STEPS - 1).astype(jnp.int32)
    return dict(activations=activations, w_qkv=w_qkv, w_out=w_out, stash=stash, qk_gain=qk_gain, modulation=modulation, patch_slot=patch_slot, timestep=timestep)


epsilon = 1e-06

def rms_norm(entries, gain):
    mean_square = lax.optimization_barrier(jnp.mean(entries * entries, axis=-1, keepdims=True))
    return entries * lax.rsqrt(mean_square + epsilon) * gain

def attend(triple_in):
    queries, keys_in, vals_in = triple_in
    scores = jnp.dot(queries, keys_in.T, preferred_element_type=jnp.float32) * (1.0 / math.sqrt(HD))
    weights = jnp.exp(scores)
    probabilities = (weights / lax.optimization_barrier(jnp.sum(weights, axis=-1, keepdims=True))).astype(jnp.bfloat16)
    return jnp.dot(probabilities, vals_in, preferred_element_type=jnp.float32).astype(jnp.bfloat16)

def by_head(tensor, length):
    return jnp.transpose(tensor, (0, 2, 1, 3)).reshape(2 * HEADS, length, HD)

def pick_step(pair_in):
    table, step_now = pair_in
    return lax.dynamic_index_in_dim(table, step_now.astype(jnp.int32), 0, keepdims=False)

def run_section(section_in):
    acts, qkv_weight, out_weight, stash_now, gains, modulate, slot = section_in
    as_float = acts.astype(jnp.float32)
    row_mean = lax.optimization_barrier(jnp.mean(as_float, axis=-1, keepdims=True))
    row_var = lax.optimization_barrier(jnp.mean(jnp.square(as_float - row_mean), axis=-1, keepdims=True))
    normed = ((as_float - row_mean) * lax.rsqrt(row_var + epsilon) * (1.0 + modulate[1]) + modulate[0]).astype(jnp.bfloat16)
    mixed_qkv = jnp.dot(normed.reshape(2 * PATCH, D), qkv_weight.reshape(D, 3 * HEADS * HD), preferred_element_type=jnp.float32)
    mixed_qkv = mixed_qkv.reshape(2, PATCH, 3, HEADS, HD)
    queries = rms_norm(mixed_qkv[:, :, 0], gains[0]).astype(jnp.bfloat16)
    fresh_keys = mixed_qkv[:, :, 1].astype(jnp.bfloat16).reshape(2, PATCH, HEADS * HD)
    fresh_vals = mixed_qkv[:, :, 2].astype(jnp.bfloat16).reshape(2, PATCH, HEADS * HD)
    offset_row = (slot * PATCH).astype(jnp.int32)
    zero_index = jnp.zeros((), jnp.int32)
    keys_all = lax.dynamic_update_slice(stash_now[:, 0], fresh_keys, (zero_index, offset_row, zero_index))
    vals_all = lax.dynamic_update_slice(stash_now[:, 1], fresh_vals, (zero_index, offset_row, zero_index))
    keys_normed = rms_norm(keys_all.astype(jnp.float32).reshape(2, STASH, HEADS, HD), gains[1]).astype(jnp.bfloat16)
    vals_heads = vals_all.reshape(2, STASH, HEADS, HD)
    attn = lax.map(attend, (by_head(queries, PATCH), by_head(keys_normed, STASH), by_head(vals_heads, STASH)))
    attn_rows = jnp.transpose(attn.reshape(2, HEADS, PATCH, HD), (0, 2, 1, 3)).reshape(2 * PATCH, HEADS * HD)
    groups = N_CFG * N_SP
    group_cols = HEADS * HD // groups
    projected = jnp.zeros((2 * PATCH, D), jnp.float32)
    for index_g in range(groups):
        lower = index_g * group_cols
        partial_term = jnp.dot(attn_rows[:, lower:lower + group_cols], out_weight[lower:lower + group_cols], preferred_element_type=jnp.float32).astype(jnp.bfloat16)
        projected = projected + lax.optimization_barrier(partial_term).astype(jnp.float32)
    mixed = as_float.reshape(2 * PATCH, D) + modulate[2] * projected
    return mixed.astype(jnp.bfloat16).reshape(2, PATCH, D)

def reference(activations, w_qkv, w_out, stash, qk_gain, modulation, patch_slot, timestep):
    modulate_rows = lax.map(pick_step, (modulation, timestep)).astype(jnp.float32)
    outputs = lax.map(run_section, (activations, w_qkv, w_out, stash, qk_gain, modulate_rows, patch_slot))
    return jnp.roll(outputs, 1, axis=0)
```

```python
import functools
import math

import jax
import jax.numpy as jnp
from jax import lax
from jax.experimental import pallas as pl
from jax.experimental.pallas import tpu as pltpu
from jax.sharding import PartitionSpec as P

EPS = 1e-06
BF = jnp.bfloat16
F32 = jnp.float32
VMEM = pl.BlockSpec(memory_space=pltpu.VMEM)
SMEM = pl.BlockSpec(memory_space=pltpu.SMEM)


def shift(value, axis, steps):
    count = lax.axis_size(axis)
    return lax.ppermute(value, axis, [(i, (i + steps) % count) for i in range(count)])


def call(body, outs, args, specs, flops=0, exps=0, name=None):
    nbytes = sum(math.prod(a.shape) * a.dtype.itemsize for a in args)
    return pl.pallas_call(
        body,
        out_shape=[jax.ShapeDtypeStruct(s, d) for s, d in outs],
        in_specs=specs,
        out_specs=[VMEM] * len(outs),
        compiler_params=pltpu.CompilerParams(vmem_limit_bytes=48 * 1024 * 1024),
        cost_estimate=pl.CostEstimate(flops=flops, bytes_accessed=nbytes, transcendentals=exps),
        name=name,
    )(*args)


def norm_body(step_ref, act_ref, mod_ref, *out_refs):
    steps = mod_ref.shape[1]
    pick = lax.broadcasted_iota(jnp.int32, (steps, 1), 0) == step_ref[0]

    def row(j):
        return jnp.sum(jnp.where(pick, mod_ref[j].astype(F32), 0.0), axis=0, keepdims=True)

    pieces = out_refs[:-1]
    part = pieces[0].shape[0]
    for r, piece in enumerate(pieces):
        a = act_ref[r * part : (r + 1) * part, :].astype(F32)
        mean = jnp.mean(a, axis=-1, keepdims=True)
        a = a - mean
        var = jnp.mean(a * a, axis=-1, keepdims=True)
        piece[...] = (a * lax.rsqrt(var + EPS) * (1.0 + row(1)) + row(0)).astype(BF)
    out_refs[-1][...] = row(2)


def keys_body(own_ref, other_ref, gain_ref, out_ref):
    gain = gain_ref[1:2, :]
    for h, ref in enumerate((own_ref, other_ref)):
        for b in range(8):
            n = ref.shape[1] // 8
            k = ref[0, b * n : (b + 1) * n, :].astype(F32)
            ms = jnp.mean(k * k, axis=-1, keepdims=True)
            out_ref[h, b * n : (b + 1) * n, :] = (k * lax.rsqrt(ms + EPS) * gain).astype(BF)


def qkv_body(count, scale, *refs):
    xs, (w0, w1, gain_ref), (q_ref, k_ref, v_ref) = refs[:count], refs[count : count + 3], refs[count + 3 :]
    x = jnp.concatenate([r[...] for r in xs], axis=0) if count > 1 else xs[0][...]

    def norm(u, g):
        ms = jnp.mean(u * u, axis=-1, keepdims=True)
        return u * lax.rsqrt(ms + EPS) * g

    hd = w0.shape[2]
    for j, out in enumerate((q_ref, k_ref, v_ref)):
        w = jnp.concatenate([w0[j], w1[j]], axis=-1)
        y = jnp.dot(x, w, preferred_element_type=F32)
        for h in range(2):
            u = y[:, h * hd : (h + 1) * hd]
            if j == 0:
                out[h] = (norm(u, gain_ref[0:1, :]) * scale).astype(BF)
            elif j == 1:
                out[h] = norm(u.astype(BF).astype(F32), gain_ref[1:2, :]).astype(BF)
            else:
                out[h] = u.astype(BF)


def block_sum(q, k, v):
    s = lax.dot_general(q, k, (((1,), (1,)), ((), ())), preferred_element_type=F32)
    p = jnp.exp2(s).astype(BF)
    v = jnp.concatenate([v, jnp.ones_like(v)], axis=-1)
    return jnp.dot(p, v, preferred_element_type=F32)


def stale_body(patch, slot_ref, q_ref, kn_ref, own_ref, other_ref, acc_ref):
    slot = slot_ref[0]
    blocks = kn_ref.shape[1] // patch
    for h, ref in enumerate((own_ref, other_ref)):
        q = q_ref[h]
        acc = None
        for i in range(blocks - 1):
            at = pl.ds(pl.multiple_of((i + (slot <= i).astype(jnp.int32)) * patch, patch), patch)
            t = block_sum(q, kn_ref[h, at, :], ref[1, at, :])
            acc = t if acc is None else acc + t
        acc_ref[h] = acc


def finish_body(groups, q_ref, acc_ref, *refs):
    ks, vs = refs[:groups], refs[groups : 2 * groups]
    w0, w1 = refs[2 * groups : 2 * groups + 2]
    outs = refs[2 * groups + 2 :]
    heads = []
    hd = q_ref.shape[2]
    for h in range(2):
        q = q_ref[h]
        k = jnp.concatenate([r[h] for r in ks], axis=0)
        v = jnp.concatenate([r[h] for r in vs], axis=0)
        acc = acc_ref[h] + block_sum(q, k, v)
        heads.append((acc[:, :hd] / acc[:, hd:]).astype(BF))
    attn = jnp.concatenate(heads, axis=-1)
    w = jnp.concatenate([w0[...], w1[...]], axis=0)
    lo = 0
    full = jnp.dot(attn, w, preferred_element_type=F32).astype(BF)
    for out in outs:
        n = out.shape[0]
        out[...] = full[lo : lo + n]
        lo += n


def shards(activations, w_qkv, w_out, stash, qk_gain, modulation, patch_slot, timestep):
    rows, width = activations.shape[2:]
    hd = qk_gain.shape[2]
    n_sp = lax.axis_size("sp")
    patch = rows * n_sp
    stash_len = stash.shape[3]
    pieces = 2
    part = rows // pieces
    half = part // 2
    core = lax.axis_index("cfg")
    gain = qk_gain[0]

    acts = activations[0, 0]
    mod = jnp.transpose(modulation[0], (1, 0, 2))
    *own, gate = call(
        norm_body,
        [((part, width), BF)] * pieces + [((1, width), F32)],
        (timestep, acts, mod),
        [SMEM, VMEM, VMEM],
        flops=rows * width * 10,
        name="norm",
    )
    w_own = jnp.transpose(w_qkv[0], (1, 0, 2))
    w_other = shift(w_own, "cfg", 1)
    kv_own = lax.dynamic_index_in_dim(stash[0], core, 0, keepdims=False)
    kv_other = shift(lax.dynamic_index_in_dim(stash[0], 1 - core, 0, keepdims=False), "cfg", 1)
    wo_own = w_out[0]
    wo_other = shift(wo_own, "cfg", 1)

    ups, downs = [list(own)], [list(own)]
    for k in range(1, 4):
        ups.append([shift(v, "sp", 1) for v in ups[-1]])
        downs.append([shift(v, "sp", -1) for v in downs[-1]])
    last = []
    for r in range(pieces):
        last.append(shift(ups[3][r][:half], "sp", 1))
        last.append(shift(downs[3][r][half:], "sp", -1))
    groups = [list(own)] + [ups[k] + downs[k] for k in range(1, 4)] + [last]

    (kn,) = call(
        keys_body,
        [((2, stash_len, hd), BF)],
        (kv_own, kv_other, gain),
        [VMEM] * 3,
        flops=2 * stash_len * hd * 6,
        name="keys",
    )
    scale = 1.0 / math.sqrt(hd) / math.log(2.0)
    qs, ks, vs, accs = [], [], [], []
    for xs in groups:
        m = sum(x.shape[0] for x in xs)
        q, k, v = call(
            functools.partial(qkv_body, len(xs), scale),
            [((2, m, hd), BF)] * 3,
            (*xs, w_own, w_other, gain),
            [VMEM] * (len(xs) + 3),
            flops=2 * m * width * 6 * hd,
            name="qkv",
        )
        (acc,) = call(
            functools.partial(stale_body, patch),
            [((2, m, 2 * hd), F32)],
            (patch_slot, q, kn, kv_own, kv_other),
            [SMEM] + [VMEM] * 4,
            flops=8 * m * stash_len * hd,
            exps=2 * m * stash_len,
            name="stale",
        )
        qs.append(q)
        ks.append(k)
        vs.append(v)
        accs.append(acc)

    def finish(g):
        sizes = [x.shape[0] for x in groups[g]]
        m = sum(sizes)
        return call(
            functools.partial(finish_body, len(groups)),
            [((n, width), BF) for n in sizes],
            (qs[g], accs[g], *ks, *vs, wo_own, wo_other),
            [VMEM] * (4 + 2 * len(groups)),
            flops=2 * m * width * 2 * hd,
            exps=2 * m * patch,
            name="finish",
        )

    part4 = finish(4)
    up = [shift(part4[2 * r], "sp", 1) for r in range(pieces)]
    down = [shift(part4[2 * r + 1], "sp", -1) for r in range(pieces)]

    def plus(a, b):
        return (a.astype(F32) + b.astype(F32)).astype(BF)

    for k in (3, 2, 1):
        mine = finish(k)
        to_down, to_up = mine[:pieces], mine[pieces:]
        if k == 3:
            up = [jnp.concatenate([plus(a, b[:half]), b[half:]], axis=0) for a, b in zip(up, to_up)]
            down = [jnp.concatenate([b[:half], plus(a, b[half:])], axis=0) for a, b in zip(down, to_down)]
        else:
            up = [plus(a, b) for a, b in zip(up, to_up)]
            down = [plus(a, b) for a, b in zip(down, to_down)]
        up = [shift(a, "sp", 1) for a in up]
        down = [shift(a, "sp", -1) for a in down]
    mine = finish(0)
    handed = []
    for r in range(pieces):
        total = up[r].astype(F32) + down[r].astype(F32) + mine[r].astype(F32)
        mixed = acts[r * part : (r + 1) * part].astype(F32) + gate * total
        handed.append(shift(mixed.astype(BF), "pipe", 1))
    return jnp.concatenate(handed, axis=0)[None, None]


def solution(mesh):
    return jax.shard_map(
        shards,
        mesh=mesh,
        in_specs=(
            P("pipe", "cfg", "sp", None),
            P("pipe", None, None, ("cfg", "sp")),
            P("pipe", ("cfg", "sp"), None),
            P("pipe", None, None, None, ("cfg", "sp")),
            P("pipe", None, None),
            P("pipe", None, None, None),
            P("pipe"),
            P("pipe"),
        ),
        out_specs=P("pipe", "cfg", "sp", None),
        check_vma=False,
    )
```

```python
import functools
import math

import jax
import jax.numpy as jnp
from jax import lax
from jax.experimental import pallas as pl
from jax.experimental.pallas import tpu as pltpu
from jax.sharding import PartitionSpec as P

EPS = 1e-06
BF = jnp.bfloat16
F32 = jnp.float32
VMEM = pl.BlockSpec(memory_space=pltpu.VMEM)
SMEM = pl.BlockSpec(memory_space=pltpu.SMEM)
ANY = pl.BlockSpec(memory_space=pl.ANY)


def shift(value, axis, steps):
    count = lax.axis_size(axis)
    return lax.ppermute(value, axis, [(i, (i + steps) % count) for i in range(count)])


def call(body, outs, args, specs, flops=0, exps=0, name=None, vmem=20, scratch=()):
    nbytes = sum(math.prod(a.shape) * a.dtype.itemsize for a in args)
    return pl.pallas_call(
        body,
        out_shape=[jax.ShapeDtypeStruct(s, d) for s, d in outs],
        in_specs=specs,
        out_specs=[VMEM] * len(outs),
        scratch_shapes=list(scratch),
        compiler_params=pltpu.CompilerParams(vmem_limit_bytes=vmem << 20),
        cost_estimate=pl.CostEstimate(flops=flops, bytes_accessed=nbytes, transcendentals=exps),
        name=name,
    )(*args)


def norm_body(step_ref, act_hbm, mod_hbm, one_ref, two_ref, gate_ref, act_ref, mod_ref, sems):
    copies = [
        pltpu.make_async_copy(mod_hbm, mod_ref, sems.at[0]),
        pltpu.make_async_copy(act_hbm, act_ref, sems.at[1]),
    ]
    for copy in copies:
        copy.start()
    copies[0].wait()
    steps = mod_ref.shape[1]
    pick = lax.broadcasted_iota(jnp.int32, (steps, 1), 0) == step_ref[0]

    def row(j):
        return jnp.sum(jnp.where(pick, mod_ref[j].astype(F32), 0.0), axis=0, keepdims=True)

    offset, scale = row(0), 1.0 + row(1)
    gate_ref[...] = row(2)
    copies[1].wait()
    part = one_ref.shape[0]
    for r, piece in enumerate((one_ref, two_ref)):
        a = act_ref[r * part : (r + 1) * part, :].astype(F32)
        mean = jnp.mean(a, axis=-1, keepdims=True)
        a = a - mean
        var = jnp.mean(a * a, axis=-1, keepdims=True)
        piece[...] = (a * lax.rsqrt(var + EPS) * scale + offset).astype(BF)


def stash_body(branch_ref, stash_hbm, gain_ref, out_ref, raw_ref, sems):
    branch = branch_ref[0]
    keys = pltpu.make_async_copy(stash_hbm.at[branch, 0], raw_ref, sems.at[0])
    vals = pltpu.make_async_copy(stash_hbm.at[branch, 1], out_ref.at[1], sems.at[1])
    keys.start()
    vals.start()
    gain = gain_ref[1:2, :]
    n = raw_ref.shape[0] // 8
    keys.wait()
    for b in range(8):
        k = raw_ref[b * n : (b + 1) * n, :].astype(F32)
        ms = jnp.mean(k * k, axis=-1, keepdims=True)
        out_ref[0, b * n : (b + 1) * n, :] = (k * lax.rsqrt(ms + EPS) * gain).astype(BF)
    vals.wait()


def qkv_body(count, scale, *refs):
    xs, (w0, w1, gain_ref), (q_ref, k_ref, v_ref) = refs[:count], refs[count : count + 3], refs[count + 3 :]
    x = jnp.concatenate([r[...] for r in xs], axis=0) if count > 1 else xs[0][...]

    def norm(u, g):
        ms = jnp.mean(u * u, axis=-1, keepdims=True)
        return u * lax.rsqrt(ms + EPS) * g

    hd = w0.shape[2]
    for j, out in enumerate((q_ref, k_ref, v_ref)):
        w = jnp.concatenate([w0[j], w1[j]], axis=-1)
        y = jnp.dot(x, w, preferred_element_type=F32)
        for h in range(2):
            u = y[:, h * hd : (h + 1) * hd]
            if j == 0:
                out[h] = (norm(u, gain_ref[0:1, :]) * scale).astype(BF)
            elif j == 1:
                out[h] = norm(u.astype(BF).astype(F32), gain_ref[1:2, :]).astype(BF)
            else:
                out[h] = u.astype(BF)


def block_sum(q, k, v):
    s = lax.dot_general(q, k, (((1,), (1,)), ((), ())), preferred_element_type=F32)
    p = jnp.exp2(s).astype(BF)
    v = jnp.concatenate([v, jnp.ones_like(v)], axis=-1)
    return jnp.dot(p, v, preferred_element_type=F32)


def stale_body(patch, heads, parts, slot_ref, *refs):
    qs, kvs, outs = refs[:parts], refs[parts : parts + 2], refs[parts + 2 :]
    slot = slot_ref[0]
    for out, h in zip(outs, heads):
        kv = kvs[h]
        q = jnp.concatenate([r[h] for r in qs], axis=0)
        acc = None
        for b in range(kv.shape[1] // patch - 1):
            at = pl.ds(pl.multiple_of((b + (slot <= b).astype(jnp.int32)) * patch, patch), patch)
            t = block_sum(q, kv[0, at, :], kv[1, at, :])
            acc = t if acc is None else acc + t
        out[...] = acc


def finish_body(groups, parts, *refs):
    qs, refs = refs[:parts], refs[parts:]
    accs, refs = refs[:2], refs[2:]
    ks, vs = refs[:groups], refs[groups : 2 * groups]
    w0, w1 = refs[2 * groups : 2 * groups + 2]
    outs = refs[2 * groups + 2 :]
    heads = []
    hd = w0.shape[0]
    for h, acc_ref in enumerate(accs):
        q = jnp.concatenate([r[h] for r in qs], axis=0)
        k = jnp.concatenate([r[h] for r in ks], axis=0)
        v = jnp.concatenate([r[h] for r in vs], axis=0)
        acc = acc_ref[...] + block_sum(q, k, v)
        heads.append((acc[:, :hd] / acc[:, hd:]).astype(BF))
    attn = jnp.concatenate(heads, axis=-1)
    w = jnp.concatenate([w0[...], w1[...]], axis=0)
    lo = 0
    full = jnp.dot(attn, w, preferred_element_type=F32).astype(BF)
    for out in outs:
        n = out.shape[0]
        out[...] = full[lo : lo + n]
        lo += n


def after(value, *others):
    return lax.optimization_barrier((value, *others))[0]


def both(one, two, *others):
    return lax.optimization_barrier((one, two, *others))[:2]


def shards(activations, w_qkv, w_out, stash, qk_gain, modulation, patch_slot, timestep):
    rows, width = activations.shape[2:]
    hd = qk_gain.shape[2]
    n_sp = lax.axis_size("sp")
    patch = rows * n_sp
    stash_len = stash.shape[3]
    part = rows // 2
    core = lax.axis_index("cfg")
    gain = qk_gain[0]

    acts = activations[0, 0]
    mod = jnp.transpose(modulation[0], (1, 0, 2))
    own0, own1, gate = call(
        norm_body,
        [((part, width), BF)] * 2 + [((1, width), F32)],
        (timestep, acts, mod),
        [SMEM, ANY, ANY],
        flops=rows * width * 10,
        name="norm",
        scratch=(
            pltpu.VMEM(acts.shape, BF),
            pltpu.VMEM(mod.shape, BF),
            pltpu.SemaphoreType.DMA((2,)),
        ),
        vmem=60,
    )

    def up(v):
        return shift(v, "sp", 1)

    def down(v):
        return shift(v, "sp", -1)

    w_own = jnp.transpose(w_qkv[0], (1, 0, 2))
    wo_own = w_out[0]
    scale = 1.0 / math.sqrt(hd) / math.log(2.0)

    def qkv(xs):
        m = sum(x.shape[0] for x in xs)
        return call(
            functools.partial(qkv_body, len(xs), scale),
            [((2, m, hd), BF)] * 3,
            (*xs, w_own, w_other, gain),
            [VMEM] * (len(xs) + 3),
            flops=2 * m * width * 6 * hd,
            name="qkv",
        )

    def stale(qs, heads):
        m = sum(q.shape[1] for q in qs)
        return call(
            functools.partial(stale_body, patch, heads, len(qs)),
            [((m, 2 * hd), F32)] * len(heads),
            (patch_slot, *qs, kv_own, kv_other),
            [SMEM] + [VMEM] * (len(qs) + 2),
            flops=4 * m * stash_len * hd * len(heads),
            exps=m * stash_len * len(heads),
            name="stale",
        )

    def stash_part(branch, *others):
        return call(
            stash_body,
            [((2, stash_len, hd), BF)],
            (branch.astype(jnp.int32)[None], after(stash[0], *others), gain),
            [SMEM, ANY, VMEM],
            flops=stash_len * hd * 10,
            name="stash",
            scratch=(pltpu.VMEM((stash_len, hd), BF), pltpu.SemaphoreType.DMA((2,))),
            vmem=50,
        )[0]

    u0, d1 = [up(own0)], [down(own1)]
    w_other = shift(after(w_own, own0), "cfg", 1)
    send = stash_part(1 - core, own0)
    p, q = both(own1, own0, send)
    u1, d0 = [up(p)], [down(q)]
    p, q = both(u0[0], d1[0])
    kv_other = shift(after(send, p, q), "cfg", 1)
    kv_own = stash_part(core, send, p, q)
    p, q = both(p, q, kv_own)
    u0.append(up(p))
    d1.append(down(q))
    p, q = both(u1[0], d0[0])
    wo_other = shift(after(wo_own, p, q), "cfg", 1)
    u1.append(up(p))
    d0.append(down(q))
    a_q, a_k, a_v = qkv([own0, own1, u0[0], u1[0], d0[0], d1[0]])
    p, q = both(u0[1], d1[1], a_q)
    u0.append(up(p))
    d1.append(down(q))
    b_q, b_k, b_v = qkv([u0[1], u1[1], d0[1], d1[1]])
    p, q = both(u1[1], d0[1], b_q)
    u1.append(up(p))
    d0.append(down(q))
    near = stale([a_q, b_q], [0])
    p, q = both(u0[2], d1[2], near[0])
    u0.append(up(p))
    d1.append(down(q))
    near += stale([a_q, b_q], [1])
    c_q, c_k, c_v = qkv([u0[2], u1[2], d0[2], d1[2]])
    p, q = both(u0[3], d1[3], near[1], c_q)
    d_q, d_k, d_v = qkv([p, q])
    far = stale([c_q, d_q], [0, 1])
    ks, vs = (a_k, b_k, c_k, d_k), (a_v, b_v, c_v, d_v)

    def finish(qs, acc, count):
        m = count * part
        return call(
            functools.partial(finish_body, len(ks), len(qs)),
            [((part, width), BF)] * count,
            (*qs, *acc, *ks, *vs, wo_own, wo_other),
            [VMEM] * (4 + len(qs) + 2 * len(ks)),
            flops=2 * m * width * 2 * hd,
            exps=2 * m * patch,
            name="finish",
        )

    def plus(a, b):
        return (a.astype(F32) + b.astype(F32)).astype(BF)

    *t3, far0, far1 = finish([c_q, d_q], far, 6)
    up0, dn1 = up(far0), down(far1)
    up1, dn0 = up(t3[3]), down(t3[0])
    near_out = finish([a_q, b_q], near, 10)
    t0, t1, t2 = near_out[:2], near_out[2:6], near_out[6:]
    up0, dn1 = both(up0, dn1)
    up0, dn1 = up(plus(up0, t3[2])), down(plus(dn1, t3[1]))
    up1, dn0 = both(up1, dn0)
    up1, dn0 = up(plus(up1, t2[3])), down(plus(dn0, t2[0]))
    up0, dn1 = both(up0, dn1)
    up0, dn1 = up(plus(up0, t2[2])), down(plus(dn1, t2[1]))
    up1, dn0 = both(up1, dn0)
    up1, dn0 = up(plus(up1, t1[3])), down(plus(dn0, t1[0]))
    up0, dn1 = both(up0, dn1)
    up0, dn1 = up(plus(up0, t1[2])), down(plus(dn1, t1[1]))
    handed = []
    for r, (a, b) in enumerate(((up0, dn0), (up1, dn1))):
        total = a.astype(F32) + b.astype(F32) + t0[r].astype(F32)
        mixed = acts[r * part : (r + 1) * part].astype(F32) + gate * total
        handed.append(shift(mixed.astype(BF), "pipe", 1))
    return jnp.concatenate(handed, axis=0)[None, None]


def solution(mesh):
    return jax.shard_map(
        shards,
        mesh=mesh,
        in_specs=(
            P("pipe", "cfg", "sp", None),
            P("pipe", None, None, ("cfg", "sp")),
            P("pipe", ("cfg", "sp"), None),
            P("pipe", None, None, None, ("cfg", "sp")),
            P("pipe", None, None),
            P("pipe", None, None, None),
            P("pipe"),
            P("pipe"),
        ),
        out_specs=P("pipe", "cfg", "sp", None),
        check_vma=False,
    )
```

```python
import functools
import math

import jax
import jax.numpy as jnp
from jax import lax
from jax.experimental import pallas as pl
from jax.experimental.pallas import tpu as pltpu
from jax.sharding import PartitionSpec as P

EPS = 1e-06
BF = jnp.bfloat16
F32 = jnp.float32
VMEM = pl.BlockSpec(memory_space=pltpu.VMEM)
SMEM = pl.BlockSpec(memory_space=pltpu.SMEM)
ANY = pl.BlockSpec(memory_space=pl.ANY)


def shift(value, axis, steps):
    count = lax.axis_size(axis)
    return lax.ppermute(value, axis, [(i, (i + steps) % count) for i in range(count)])


def call(body, outs, args, specs, flops=0, exps=0, name=None, vmem=20, scratch=()):
    nbytes = sum(math.prod(a.shape) * a.dtype.itemsize for a in args)
    return pl.pallas_call(
        body,
        out_shape=[jax.ShapeDtypeStruct(s, d) for s, d in outs],
        in_specs=specs,
        out_specs=[VMEM] * len(outs),
        scratch_shapes=list(scratch),
        compiler_params=pltpu.CompilerParams(vmem_limit_bytes=vmem << 20),
        cost_estimate=pl.CostEstimate(flops=flops, bytes_accessed=nbytes, transcendentals=exps),
        name=name,
    )(*args)


def norm_body(step_ref, act_hbm, mod_hbm, one_ref, two_ref, gate_ref, act_ref, mod_ref, sems):
    copies = [
        pltpu.make_async_copy(mod_hbm, mod_ref, sems.at[0]),
        pltpu.make_async_copy(act_hbm, act_ref, sems.at[1]),
    ]
    for copy in copies:
        copy.start()
    copies[0].wait()
    steps = mod_ref.shape[1]
    pick = lax.broadcasted_iota(jnp.int32, (steps, 1), 0) == step_ref[0]

    def row(j):
        return jnp.sum(jnp.where(pick, mod_ref[j].astype(F32), 0.0), axis=0, keepdims=True)

    offset, scale = row(0), 1.0 + row(1)
    gate_ref[...] = row(2)
    copies[1].wait()
    part = one_ref.shape[0]
    for r, piece in enumerate((one_ref, two_ref)):
        a = act_ref[r * part : (r + 1) * part, :].astype(F32)
        mean = jnp.mean(a, axis=-1, keepdims=True)
        a = a - mean
        var = jnp.mean(a * a, axis=-1, keepdims=True)
        piece[...] = (a * lax.rsqrt(var + EPS) * scale + offset).astype(BF)


def stash_body(branch_ref, stash_hbm, gain_ref, out_ref, raw_ref, sems):
    branch = branch_ref[0]
    keys = pltpu.make_async_copy(stash_hbm.at[branch, 0], raw_ref, sems.at[0])
    vals = pltpu.make_async_copy(stash_hbm.at[branch, 1], out_ref.at[1], sems.at[1])
    keys.start()
    vals.start()
    gain = gain_ref[1:2, :]
    n = raw_ref.shape[0] // 8
    keys.wait()
    for b in range(8):
        k = raw_ref[b * n : (b + 1) * n, :].astype(F32)
        ms = jnp.mean(k * k, axis=-1, keepdims=True)
        out_ref[0, b * n : (b + 1) * n, :] = (k * lax.rsqrt(ms + EPS) * gain).astype(BF)
    vals.wait()


def qkv_body(count, scale, *refs):
    xs, (w0, w1, gain_ref), (q_ref, k_ref, v_ref) = refs[:count], refs[count : count + 3], refs[count + 3 :]
    x = jnp.concatenate([r[...] for r in xs], axis=0) if count > 1 else xs[0][...]

    def norm(u, g):
        ms = jnp.mean(u * u, axis=-1, keepdims=True)
        return u * lax.rsqrt(ms + EPS) * g

    hd = w0.shape[2]
    for j, out in enumerate((q_ref, k_ref, v_ref)):
        w = jnp.concatenate([w0[j], w1[j]], axis=-1)
        y = jnp.dot(x, w, preferred_element_type=F32)
        for h in range(2):
            u = y[:, h * hd : (h + 1) * hd]
            if j == 0:
                out[h] = (norm(u, gain_ref[0:1, :]) * scale).astype(BF)
            elif j == 1:
                out[h] = norm(u.astype(BF).astype(F32), gain_ref[1:2, :]).astype(BF)
            else:
                out[h] = u.astype(BF)


def block_sum(q, k, v):
    s = lax.dot_general(q, k, (((1,), (1,)), ((), ())), preferred_element_type=F32)
    p = jnp.exp2(s).astype(BF)
    v = jnp.concatenate([v, jnp.ones_like(v)], axis=-1)
    return jnp.dot(p, v, preferred_element_type=F32)


def stale_body(patch, heads, parts, slot_ref, *refs):
    qs, kvs, outs = refs[:parts], refs[parts : parts + 2], refs[parts + 2 :]
    slot = slot_ref[0]
    for out, h in zip(outs, heads):
        kv = kvs[h]
        q = jnp.concatenate([r[h] for r in qs], axis=0)
        acc = None
        for b in range(kv.shape[1] // patch - 1):
            at = pl.ds(pl.multiple_of((b + (slot <= b).astype(jnp.int32)) * patch, patch), patch)
            t = block_sum(q, kv[0, at, :], kv[1, at, :])
            acc = t if acc is None else acc + t
        out[...] = acc


def finish_body(groups, parts, at, *refs):
    qs, refs = refs[:parts], refs[parts:]
    accs, refs = refs[:2], refs[2:]
    ks, vs = refs[:groups], refs[groups : 2 * groups]
    w0, w1 = refs[2 * groups : 2 * groups + 2]
    outs = refs[2 * groups + 2 :]
    heads = []
    hd = w0.shape[0]
    for h, acc_ref in enumerate(accs):
        q = jnp.concatenate([r[h] for r in qs], axis=0)
        k = jnp.concatenate([r[h] for r in ks], axis=0)
        v = jnp.concatenate([r[h] for r in vs], axis=0)
        acc = acc_ref[at : at + q.shape[0]] + block_sum(q, k, v)
        heads.append((acc[:, :hd] / acc[:, hd:]).astype(BF))
    attn = jnp.concatenate(heads, axis=-1)
    w = jnp.concatenate([w0[...], w1[...]], axis=0)
    lo = 0
    full = jnp.dot(attn, w, preferred_element_type=F32).astype(BF)
    for out in outs:
        n = out.shape[0]
        out[...] = full[lo : lo + n]
        lo += n


def after(value, *others):
    return lax.optimization_barrier((value, *others))[0]


def both(one, two, *others):
    return lax.optimization_barrier((one, two, *others))[:2]


def shards(activations, w_qkv, w_out, stash, qk_gain, modulation, patch_slot, timestep):
    rows, width = activations.shape[2:]
    hd = qk_gain.shape[2]
    n_sp = lax.axis_size("sp")
    patch = rows * n_sp
    stash_len = stash.shape[3]
    part = rows // 2
    core = lax.axis_index("cfg")
    gain = qk_gain[0]

    acts = activations[0, 0]
    mod = jnp.transpose(modulation[0], (1, 0, 2))
    own0, own1, gate = call(
        norm_body,
        [((part, width), BF)] * 2 + [((1, width), F32)],
        (timestep, acts, mod),
        [SMEM, ANY, ANY],
        flops=rows * width * 10,
        name="norm",
        scratch=(
            pltpu.VMEM(acts.shape, BF),
            pltpu.VMEM(mod.shape, BF),
            pltpu.SemaphoreType.DMA((2,)),
        ),
        vmem=60,
    )

    def up(v):
        return shift(v, "sp", 1)

    def down(v):
        return shift(v, "sp", -1)

    w_own = jnp.transpose(w_qkv[0], (1, 0, 2))
    wo_own = w_out[0]
    scale = 1.0 / math.sqrt(hd) / math.log(2.0)

    def qkv(xs):
        m = sum(x.shape[0] for x in xs)
        return call(
            functools.partial(qkv_body, len(xs), scale),
            [((2, m, hd), BF)] * 3,
            (*xs, w_own, w_other, gain),
            [VMEM] * (len(xs) + 3),
            flops=2 * m * width * 6 * hd,
            name="qkv",
        )

    def stale(qs, heads):
        m = sum(q.shape[1] for q in qs)
        return call(
            functools.partial(stale_body, patch, heads, len(qs)),
            [((m, 2 * hd), F32)] * len(heads),
            (patch_slot, *qs, kv_own, kv_other),
            [SMEM] + [VMEM] * (len(qs) + 2),
            flops=4 * m * stash_len * hd * len(heads),
            exps=m * stash_len * len(heads),
            name="stale",
        )

    def stash_part(branch, *others):
        return call(
            stash_body,
            [((2, stash_len, hd), BF)],
            (branch.astype(jnp.int32)[None], after(stash[0], *others), gain),
            [SMEM, ANY, VMEM],
            flops=stash_len * hd * 10,
            name="stash",
            scratch=(pltpu.VMEM((stash_len, hd), BF), pltpu.SemaphoreType.DMA((2,))),
            vmem=50,
        )[0]

    u0, d1 = [up(own0)], [down(own1)]
    w_other = shift(after(w_own, own0), "cfg", 1)
    send = stash_part(1 - core, own0)
    p, q = both(own1, own0, send)
    u1, d0 = [up(p)], [down(q)]
    p, q = both(u0[0], d1[0])
    kv_other = shift(send, "cfg", 1)
    kv_own = stash_part(core, send)
    p, q = both(p, q, kv_own)
    u0.append(up(p))
    d1.append(down(q))
    p, q = both(u1[0], d0[0])
    wo_other = shift(after(wo_own, p, q), "cfg", 1)
    u1.append(up(p))
    d0.append(down(q))
    a_q, a_k, a_v = qkv([own0, own1, u0[0], u1[0], d0[0], d1[0]])
    p, q = both(u0[1], d1[1], a_q)
    u0.append(up(p))
    d1.append(down(q))
    b_q, b_k, b_v = qkv([u0[1], u1[1], d0[1], d1[1]])
    p, q = both(u1[1], d0[1], b_q)
    u1.append(up(p))
    d0.append(down(q))
    near = stale([a_q, b_q], [0])
    p, q = both(u0[2], d1[2], near[0])
    u0.append(up(p))
    d1.append(down(q))
    near += stale([a_q, b_q], [1])
    c_q, c_k, c_v = qkv([u0[2], u1[2], d0[2], d1[2]])
    p, q = both(u0[3], d1[3], near[1], c_q)
    d_q, d_k, d_v = qkv([p, q])
    far = stale([c_q, d_q], [0, 1])
    ks, vs = (a_k, b_k, c_k, d_k), (a_v, b_v, c_v, d_v)

    def finish(qs, acc, count, at=0):
        m = count * part
        return call(
            functools.partial(finish_body, len(ks), len(qs), at),
            [((part, width), BF)] * count,
            (*qs, *acc, *ks, *vs, wo_own, wo_other),
            [VMEM] * (4 + len(qs) + 2 * len(ks)),
            flops=2 * m * width * 2 * hd,
            exps=2 * m * patch,
            name="finish",
        )

    def plus(a, b):
        return (a.astype(F32) + b.astype(F32)).astype(BF)

    far0, far1 = finish([d_q], far, 2, 4 * part)
    up0, dn1 = up(far0), down(far1)
    t3 = finish([after(c_q, far0)], far, 4)
    up1, dn0 = up(t3[3]), down(t3[0])
    near_out = finish([a_q, b_q], near, 10)
    t0, t1, t2 = near_out[:2], near_out[2:6], near_out[6:]
    up0, dn1 = both(up0, dn1)
    up0, dn1 = up(plus(up0, t3[2])), down(plus(dn1, t3[1]))
    up1, dn0 = both(up1, dn0)
    up1, dn0 = up(plus(up1, t2[3])), down(plus(dn0, t2[0]))
    up0, dn1 = both(up0, dn1)
    up0, dn1 = up(plus(up0, t2[2])), down(plus(dn1, t2[1]))
    up1, dn0 = both(up1, dn0)
    up1, dn0 = up(plus(up1, t1[3])), down(plus(dn0, t1[0]))
    up0, dn1 = both(up0, dn1)
    up0, dn1 = up(plus(up0, t1[2])), down(plus(dn1, t1[1]))
    handed = []
    for r, (a, b) in enumerate(((up0, dn0), (up1, dn1))):
        total = a.astype(F32) + b.astype(F32) + t0[r].astype(F32)
        mixed = acts[r * part : (r + 1) * part].astype(F32) + gate * total
        handed.append(shift(mixed.astype(BF), "pipe", 1))
    return jnp.concatenate(handed, axis=0)[None, None]


def solution(mesh):
    return jax.shard_map(
        shards,
        mesh=mesh,
        in_specs=(
            P("pipe", "cfg", "sp", None),
            P("pipe", None, None, ("cfg", "sp")),
            P("pipe", ("cfg", "sp"), None),
            P("pipe", None, None, None, ("cfg", "sp")),
            P("pipe", None, None),
            P("pipe", None, None, None),
            P("pipe"),
            P("pipe"),
        ),
        out_specs=P("pipe", "cfg", "sp", None),
        check_vma=False,
    )
```

```python
import functools
import math

import jax
import jax.numpy as jnp
from jax import lax
from jax.experimental import pallas as pl
from jax.experimental.pallas import tpu as pltpu
from jax.sharding import PartitionSpec as P

EPS = 1e-06
BF = jnp.bfloat16
F32 = jnp.float32
VMEM = pl.BlockSpec(memory_space=pltpu.VMEM)
SMEM = pl.BlockSpec(memory_space=pltpu.SMEM)
ANY = pl.BlockSpec(memory_space=pl.ANY)


def shift(value, axis, steps):
    count = lax.axis_size(axis)
    return lax.ppermute(value, axis, [(i, (i + steps) % count) for i in range(count)])


def call(body, outs, args, specs, flops=0, exps=0, name=None, vmem=20, scratch=()):
    nbytes = sum(math.prod(a.shape) * a.dtype.itemsize for a in args)
    return pl.pallas_call(
        body,
        out_shape=[jax.ShapeDtypeStruct(s, d) for s, d in outs],
        in_specs=specs,
        out_specs=[VMEM] * len(outs),
        scratch_shapes=list(scratch),
        compiler_params=pltpu.CompilerParams(vmem_limit_bytes=vmem << 20),
        cost_estimate=pl.CostEstimate(flops=flops, bytes_accessed=nbytes, transcendentals=exps),
        name=name,
    )(*args)


def norm_body(step_ref, act_hbm, mod_hbm, one_ref, two_ref, gate_ref, act_ref, mod_ref, sems):
    copies = [
        pltpu.make_async_copy(mod_hbm, mod_ref, sems.at[0]),
        pltpu.make_async_copy(act_hbm, act_ref, sems.at[1]),
    ]
    for copy in copies:
        copy.start()
    copies[0].wait()
    steps = mod_ref.shape[1]
    pick = lax.broadcasted_iota(jnp.int32, (steps, 1), 0) == step_ref[0]

    def row(j):
        return jnp.sum(jnp.where(pick, mod_ref[j].astype(F32), 0.0), axis=0, keepdims=True)

    offset, scale = row(0), 1.0 + row(1)
    gate_ref[...] = row(2)
    copies[1].wait()
    part = one_ref.shape[0]
    for r, piece in enumerate((one_ref, two_ref)):
        a = act_ref[r * part : (r + 1) * part, :].astype(F32)
        mean = jnp.mean(a, axis=-1, keepdims=True)
        a = a - mean
        var = jnp.mean(a * a, axis=-1, keepdims=True)
        piece[...] = (a * lax.rsqrt(var + EPS) * scale + offset).astype(BF)


def stash_body(branch_ref, stash_hbm, gain_hbm, out_ref, raw_ref, gain_ref, sems):
    branch = branch_ref[0]
    keys = pltpu.make_async_copy(stash_hbm.at[branch, 0], raw_ref, sems.at[0])
    vals = pltpu.make_async_copy(stash_hbm.at[branch, 1], out_ref.at[1], sems.at[1])
    gains = pltpu.make_async_copy(gain_hbm, gain_ref, sems.at[2])
    keys.start()
    vals.start()
    gains.start()
    n = raw_ref.shape[0] // 8
    gains.wait()
    gain = gain_ref[1:2, :]
    keys.wait()
    for b in range(8):
        k = raw_ref[b * n : (b + 1) * n, :].astype(F32)
        ms = jnp.mean(k * k, axis=-1, keepdims=True)
        out_ref[0, b * n : (b + 1) * n, :] = (k * lax.rsqrt(ms + EPS) * gain).astype(BF)
    vals.wait()


def qkv_body(count, scale, *refs):
    xs, (w0, w1, gain_ref), (q_ref, k_ref, v_ref) = refs[:count], refs[count : count + 3], refs[count + 3 :]
    x = jnp.concatenate([r[...] for r in xs], axis=0) if count > 1 else xs[0][...]

    def norm(u, g):
        ms = jnp.mean(u * u, axis=-1, keepdims=True)
        return u * lax.rsqrt(ms + EPS) * g

    hd = w0.shape[2]
    for j, out in enumerate((q_ref, k_ref, v_ref)):
        w = jnp.concatenate([w0[j], w1[j]], axis=-1)
        y = jnp.dot(x, w, preferred_element_type=F32)
        for h in range(2):
            u = y[:, h * hd : (h + 1) * hd]
            if j == 0:
                out[h] = (norm(u, gain_ref[0:1, :]) * scale).astype(BF)
            elif j == 1:
                out[h] = norm(u.astype(BF).astype(F32), gain_ref[1:2, :]).astype(BF)
            else:
                out[h] = u.astype(BF)


def block_sum(q, k, v):
    s = lax.dot_general(q, k, (((1,), (1,)), ((), ())), preferred_element_type=F32)
    p = jnp.exp2(s).astype(BF)
    v = jnp.concatenate([v, jnp.ones_like(v)], axis=-1)
    return jnp.dot(p, v, preferred_element_type=F32)


def stale_body(patch, heads, parts, slot_ref, *refs):
    qs, kvs, outs = refs[:parts], refs[parts : parts + 2], refs[parts + 2 :]
    slot = slot_ref[0]
    for out, h in zip(outs, heads):
        kv = kvs[h]
        q = jnp.concatenate([r[h] for r in qs], axis=0)
        acc = None
        for b in range(kv.shape[1] // patch - 1):
            at = pl.ds(pl.multiple_of((b + (slot <= b).astype(jnp.int32)) * patch, patch), patch)
            t = block_sum(q, kv[0, at, :], kv[1, at, :])
            acc = t if acc is None else acc + t
        out[...] = acc


def finish_body(groups, parts, at, *refs):
    qs, refs = refs[:parts], refs[parts:]
    accs, refs = refs[:2], refs[2:]
    ks, vs = refs[:groups], refs[groups : 2 * groups]
    w0, w1 = refs[2 * groups : 2 * groups + 2]
    outs = refs[2 * groups + 2 :]
    heads = []
    hd = w0.shape[0]
    for h, acc_ref in enumerate(accs):
        q = jnp.concatenate([r[h] for r in qs], axis=0)
        k = jnp.concatenate([r[h] for r in ks], axis=0)
        v = jnp.concatenate([r[h] for r in vs], axis=0)
        acc = acc_ref[at : at + q.shape[0]] + block_sum(q, k, v)
        heads.append((acc[:, :hd] / acc[:, hd:]).astype(BF))
    attn = jnp.concatenate(heads, axis=-1)
    w = jnp.concatenate([w0[...], w1[...]], axis=0)
    lo = 0
    full = jnp.dot(attn, w, preferred_element_type=F32).astype(BF)
    for out in outs:
        n = out.shape[0]
        out[...] = full[lo : lo + n]
        lo += n


def after(value, *others):
    return lax.optimization_barrier((value, *others))[0]


def both(one, two, *others):
    return lax.optimization_barrier((one, two, *others))[:2]


def shards(activations, w_qkv, w_out, stash, qk_gain, modulation, patch_slot, timestep):
    rows, width = activations.shape[2:]
    hd = qk_gain.shape[2]
    n_sp = lax.axis_size("sp")
    patch = rows * n_sp
    stash_len = stash.shape[3]
    part = rows // 2
    core = lax.axis_index("cfg")
    gain = qk_gain[0]

    acts = activations[0, 0]
    mod = jnp.transpose(modulation[0], (1, 0, 2))
    own0, own1, gate = call(
        norm_body,
        [((part, width), BF)] * 2 + [((1, width), F32)],
        (timestep, acts, mod),
        [SMEM, ANY, ANY],
        flops=rows * width * 10,
        name="norm",
        scratch=(
            pltpu.VMEM(acts.shape, BF),
            pltpu.VMEM(mod.shape, BF),
            pltpu.SemaphoreType.DMA((2,)),
        ),
        vmem=60,
    )

    def up(v):
        return shift(v, "sp", 1)

    def down(v):
        return shift(v, "sp", -1)

    w_own = jnp.transpose(w_qkv[0], (1, 0, 2))
    wo_own = w_out[0]
    scale = 1.0 / math.sqrt(hd) / math.log(2.0)

    def qkv(xs):
        m = sum(x.shape[0] for x in xs)
        return call(
            functools.partial(qkv_body, len(xs), scale),
            [((2, m, hd), BF)] * 3,
            (*xs, w_own, w_other, gain),
            [VMEM] * (len(xs) + 3),
            flops=2 * m * width * 6 * hd,
            name="qkv",
        )

    def stale(qs, heads):
        m = sum(q.shape[1] for q in qs)
        return call(
            functools.partial(stale_body, patch, heads, len(qs)),
            [((m, 2 * hd), F32)] * len(heads),
            (patch_slot, *qs, kv_own, kv_other),
            [SMEM] + [VMEM] * (len(qs) + 2),
            flops=4 * m * stash_len * hd * len(heads),
            exps=m * stash_len * len(heads),
            name="stale",
        )

    def stash_part(branch, *others):
        return call(
            stash_body,
            [((2, stash_len, hd), BF)],
            (branch.astype(jnp.int32)[None], after(stash[0], *others), gain),
            [SMEM, ANY, ANY],
            flops=stash_len * hd * 10,
            name="stash",
            scratch=(
                pltpu.VMEM((stash_len, hd), BF),
                pltpu.VMEM(gain.shape, F32),
                pltpu.SemaphoreType.DMA((3,)),
            ),
            vmem=50,
        )[0]

    u0, d1 = [up(own0)], [down(own1)]
    send = stash_part(1 - core, own0)
    w_other = shift(after(w_own, send), "cfg", 1)
    p, q = both(own1, own0, send)
    u1, d0 = [up(p)], [down(q)]
    p, q = both(u0[0], d1[0])
    kv_other = shift(send, "cfg", 1)
    kv_own = stash_part(core, send)
    p, q = both(p, q, kv_own)
    u0.append(up(p))
    d1.append(down(q))
    p, q = both(u1[0], d0[0])
    wo_other = shift(after(wo_own, p, q), "cfg", 1)
    u1.append(up(p))
    d0.append(down(q))
    a_q, a_k, a_v = qkv([own0, own1, u0[0], u1[0], d0[0], d1[0]])
    p, q = both(u0[1], d1[1], a_q)
    u0.append(up(p))
    d1.append(down(q))
    b_q, b_k, b_v = qkv([u0[1], u1[1], d0[1], d1[1]])
    p, q = both(u1[1], d0[1], b_q)
    u1.append(up(p))
    d0.append(down(q))
    near = stale([a_q, b_q], [0])
    p, q = both(u0[2], d1[2], near[0])
    u0.append(up(p))
    d1.append(down(q))
    near += stale([a_q, b_q], [1])
    c_q, c_k, c_v = qkv([u0[2], u1[2], d0[2], d1[2]])
    p, q = both(u0[3], d1[3], near[1], c_q)
    d_q, d_k, d_v = qkv([p, q])
    far = stale([c_q, d_q], [0, 1])
    ks, vs = (a_k, b_k, c_k, d_k), (a_v, b_v, c_v, d_v)

    def finish(qs, acc, count, at=0):
        m = count * part
        return call(
            functools.partial(finish_body, len(ks), len(qs), at),
            [((part, width), BF)] * count,
            (*qs, *acc, *ks, *vs, wo_own, wo_other),
            [VMEM] * (4 + len(qs) + 2 * len(ks)),
            flops=2 * m * width * 2 * hd,
            exps=2 * m * patch,
            name="finish",
        )

    def plus(a, b):
        return (a.astype(F32) + b.astype(F32)).astype(BF)

    far0, far1 = finish([d_q], far, 2, 4 * part)
    up0, dn1 = up(far0), down(far1)
    t3 = finish([after(c_q, far0)], far, 4)
    up1, dn0 = up(t3[3]), down(t3[0])
    near_out = finish([a_q, b_q], near, 10)
    t0, t1, t2 = near_out[:2], near_out[2:6], near_out[6:]
    up0, dn1 = both(up0, dn1)
    up0, dn1 = up(plus(up0, t3[2])), down(plus(dn1, t3[1]))
    up1, dn0 = both(up1, dn0)
    up1, dn0 = up(plus(up1, t2[3])), down(plus(dn0, t2[0]))
    up0, dn1 = both(up0, dn1)
    up0, dn1 = up(plus(up0, t2[2])), down(plus(dn1, t2[1]))
    up1, dn0 = both(up1, dn0)
    up1, dn0 = up(plus(up1, t1[3])), down(plus(dn0, t1[0]))
    up0, dn1 = both(up0, dn1)
    up0, dn1 = up(plus(up0, t1[2])), down(plus(dn1, t1[1]))
    handed = []
    for r, (a, b) in enumerate(((up0, dn0), (up1, dn1))):
        total = a.astype(F32) + b.astype(F32) + t0[r].astype(F32)
        mixed = acts[r * part : (r + 1) * part].astype(F32) + gate * total
        handed.append(shift(mixed.astype(BF), "pipe", 1))
    return jnp.concatenate(handed, axis=0)[None, None]


def solution(mesh):
    return jax.shard_map(
        shards,
        mesh=mesh,
        in_specs=(
            P("pipe", "cfg", "sp", None),
            P("pipe", None, None, ("cfg", "sp")),
            P("pipe", ("cfg", "sp"), None),
            P("pipe", None, None, None, ("cfg", "sp")),
            P("pipe", None, None),
            P("pipe", None, None, None),
            P("pipe"),
            P("pipe"),
        ),
        out_specs=P("pipe", "cfg", "sp", None),
        check_vma=False,
    )
```
